128 devices in a mesh: lat: 8 (over z_lo, y), lon: 16 (over x, z_hi, core).
Axes of the slice: x: 4, y: 4, z: 4 (z_hi: 2, z_lo: 2; z = z_hi * 2 + z_lo), core: 2. Of those that a mesh axis runs over, the one named last changes fastest.
Arguments:
- fine_tokens: bfloat16 [2, 192, 768, 512], P(None, 'lat', 'lon'), may hold values from -6 to 6
- shift_lat: int32 [1], replicated, may hold values from 1 to 5
- shift_lon: int32 [1], replicated, may hold values from 1 to 11
- rel_bias: float32 [8, 144, 144], replicated, may hold values from -6 to 270
- w_qkv: bfloat16 [512, 1536], replicated, may hold values from -0.25 to 0.25
- w_out: bfloat16 [512, 512], replicated, may hold values from -0.25 to 0.25
- w_up: bfloat16 [512, 2048], replicated, may hold values from -0.25 to 0.25
- w_down: bfloat16 [2048, 512], replicated, may hold values from -0.125 to 0.125
- w_merge: bfloat16 [2048, 1024], replicated, may hold values from -0.125 to 0.125
- w_inner: bfloat16 [1024, 4096], P('lon'), may hold values from -0.1875 to 0.1875
- w_outer: bfloat16 [4096, 1024], P('lon'), may hold values from -0.09375 to 0.09375
Outputs:
- fine_out: bfloat16 [2, 192, 768, 512], P(None, 'lat', 'lon')
- middle: bfloat16 [2, 96, 384, 1024], P(None, 'lat', 'lon')
The draws below stay inside these ranges and needn't reach their ends.
All inputs are finite; a program needn't handle non-finite values.
Results may differ from the reference program's by a relative error of at most 0.015.
Values may be sent and summed in bfloat16 or wider, within the bound.
A program may use at most 192 MiB of HBM per device.

```python
import jax
import jax.numpy as jnp
from jax import lax

D = 512
HEADS = 8
FF = 2048
D2 = 1024
FF2 = 4096
LEVELS = 2
WLAT = 6
WLON = 12
WT = 144
NLAT = 192
NLON = 768


def draw_rel_bias(key, part):
    key = jax.random.fold_in(key, 11)
    keys = jax.random.split(key, 1)
    shape = (HEADS, WT, WT)
    return jnp.clip(jax.random.normal(keys[0], shape, jnp.float32), -6.0, 6.0)


def level_of(rng, extent, shards, low, high):
    def one(axis_at, parts):
        draws = jax.random.uniform(jax.random.fold_in(jax.random.fold_in(rng, 6), axis_at), (parts,), jnp.float32, low / len(shards), high / len(shards))
        return jnp.repeat(jnp.exp(draws), extent[axis_at] // parts).reshape((-1,) + (1,) * (len(extent) - axis_at - 1))

    factor_of = one(*shards[0])
    for cut in shards[1:]:
        factor_of = factor_of * one(*cut)
    return factor_of


def noise(stream_key, dims, scale, most, cuts=(), kind=jnp.bfloat16):
    gain = level_of(stream_key, dims, cuts, -0.22, 0.18) if cuts else 1.0
    values = jax.random.normal(stream_key, dims, jnp.float32) * scale * gain
    return jnp.minimum(jnp.maximum(values, -most), most).astype(kind)


def setup_inputs(seed: int = 0) -> dict:
    streams_of = jax.random.split(jax.random.key(seed), 12)
    fine_tokens = noise(streams_of[0], (LEVELS, NLAT, NLON, D), 1.0, 6.0, ((1, 8), (2, 16)))
    shift_lat = jax.random.randint(streams_of[1], (1,), 1, WLAT).astype(jnp.int32)
    shift_lon = jax.random.randint(streams_of[2], (1,), 1, WLON).astype(jnp.int32)
    rel_bias = draw_rel_bias(jax.random.fold_in(streams_of[11], 71), 0)
    w_qkv = noise(streams_of[4], (D, 3 * D), D ** -0.5, 0.25)
    w_out = noise(streams_of[5], (D, D), D ** -0.5, 0.25)
    w_up = noise(streams_of[6], (D, FF), D ** -0.5, 0.25)
    w_down = noise(streams_of[7], (FF, D), FF ** -0.5, 0.125)
    w_merge = noise(streams_of[8], (4 * D, D2), (4 * D) ** -0.5, 0.125)
    w_inner = noise(streams_of[9], (D2, FF2), D2 ** -0.5, 0.1875, ((0, 16),))
    w_outer = noise(streams_of[10], (FF2, D2), FF2 ** -0.5, 0.09375, ((0, 16),))
    return {"fine_tokens": fine_tokens, "shift_lat": shift_lat, "shift_lon": shift_lon, "rel_bias": rel_bias, "w_qkv": w_qkv, "w_out": w_out, "w_up": w_up, "w_down": w_down, "w_merge": w_merge, "w_inner": w_inner, "w_outer": w_outer}


def layer_norm(values):
    average = lax.optimization_barrier(jnp.mean(values, axis=-1, keepdims=True))
    centered = values - average
    spread = lax.optimization_barrier(jnp.mean(centered * centered, axis=-1, keepdims=True))
    return centered * lax.rsqrt(spread + 1e-05)

def to_windows(window_grid):
    levels, lat_rows, lon_cols, feat_width = window_grid.shape
    row_blocks = lat_rows // WLAT
    col_blocks = lon_cols // WLON
    shaped = window_grid.reshape(levels, row_blocks, WLAT, col_blocks, WLON, feat_width)
    return shaped.transpose(1, 3, 0, 2, 4, 5).reshape(row_blocks * col_blocks, levels * WLAT * WLON, feat_width)

def from_windows(windows, lat_rows, lon_cols):
    row_blocks = lat_rows // WLAT
    col_blocks = lon_cols // WLON
    feat_width = windows.shape[-1]
    shaped = windows.reshape(row_blocks, col_blocks, LEVELS, WLAT, WLON, feat_width)
    return shaped.transpose(2, 0, 3, 1, 4, 5).reshape(LEVELS, lat_rows, lon_cols, feat_width)

def window_attention(windows, labels, w_qkv, w_out, rel_bias):
    win_count, win_tokens, model_width = windows.shape
    head_count = rel_bias.shape[0]
    head_size = model_width // head_count
    projected = jnp.einsum('wtd,de->wte', windows.astype(jnp.float32), w_qkv.astype(jnp.float32)).astype(jnp.bfloat16)
    queries = projected[..., :model_width].reshape(win_count, win_tokens, head_count, head_size)
    key_vecs = projected[..., model_width:2 * model_width].reshape(win_count, win_tokens, head_count, head_size)
    values = projected[..., 2 * model_width:].reshape(win_count, win_tokens, head_count, head_size)
    scores = jnp.einsum('wqhc,wkhc->whqk', queries.astype(jnp.float32), key_vecs.astype(jnp.float32))
    scores = scores * head_size ** (-0.5) + rel_bias[None]
    same_label = labels[:, :, None] == labels[:, None, :]
    scores = jnp.where(same_label[:, None], scores, -1e+30)
    scores = scores - lax.optimization_barrier(jnp.max(scores, axis=-1, keepdims=True))
    exponent = jnp.exp(scores)
    weights = (exponent / lax.optimization_barrier(jnp.sum(exponent, axis=-1, keepdims=True))).astype(jnp.bfloat16)
    context = jnp.einsum('whqk,wkhc->wqhc', weights.astype(jnp.float32), values.astype(jnp.float32))
    context = context.astype(jnp.bfloat16).reshape(win_count, win_tokens, model_width)
    return jnp.einsum('wtd,de->wte', context.astype(jnp.float32), w_out.astype(jnp.float32)).astype(jnp.bfloat16)

def fine_block(tokens_block, restored_block, w_up, w_down):
    residual_sum = tokens_block.astype(jnp.float32) + restored_block.astype(jnp.float32)
    feat_width = residual_sum.shape[-1]
    flat_sum = residual_sum.reshape(-1, feat_width)
    normed = layer_norm(flat_sum).astype(jnp.bfloat16)
    hidden = jax.nn.gelu(jnp.dot(normed, w_up, preferred_element_type=jnp.float32), approximate=False).astype(jnp.bfloat16)
    result = flat_sum + jnp.dot(hidden, w_down, preferred_element_type=jnp.float32)
    return result.astype(jnp.bfloat16).reshape(residual_sum.shape)

def middle_block(merged_block, w_merge, w_inner, w_outer):
    shape_in = merged_block.shape
    flat_in = merged_block.reshape(-1, shape_in[-1])
    coarse = jnp.dot(layer_norm(flat_in.astype(jnp.float32)).astype(jnp.bfloat16), w_merge, preferred_element_type=jnp.float32).astype(jnp.bfloat16)
    coarse_norm = layer_norm(coarse.astype(jnp.float32)).astype(jnp.bfloat16)
    inner_act = jax.nn.gelu(jnp.dot(coarse_norm, w_inner, preferred_element_type=jnp.float32), approximate=False).astype(jnp.bfloat16)
    result = coarse.astype(jnp.float32) + jnp.dot(inner_act, w_outer, preferred_element_type=jnp.float32)
    return result.astype(jnp.bfloat16).reshape(shape_in[:-1] + (w_outer.shape[1],))

def reference(fine_tokens, shift_lat, shift_lon, rel_bias, w_qkv, w_out, w_up, w_down, w_merge, w_inner, w_outer):
    lat_shift = shift_lat[0].astype(jnp.int32)
    lon_shift = shift_lon[0].astype(jnp.int32)
    zero_index = jnp.zeros((), jnp.int32)
    normed = layer_norm(fine_tokens.astype(jnp.float32)).astype(jnp.bfloat16)
    taller = jnp.concatenate([normed, normed[:, :WLAT]], axis=1)
    wider = jnp.concatenate([taller, taller[:, :, :WLON]], axis=2)
    rolled = lax.dynamic_slice(wider, (zero_index, lat_shift, lon_shift, zero_index), (LEVELS, NLAT, NLON, D))
    row_index = lax.broadcasted_iota(jnp.int32, (LEVELS, NLAT, NLON, 1), 1)
    labels = (row_index + lat_shift >= NLAT).astype(jnp.int32)
    row_blocks = NLAT // WLAT
    col_blocks = NLON // WLON
    win_all = to_windows(rolled).reshape(row_blocks, col_blocks, WT, D)
    label_all = to_windows(labels).reshape(row_blocks, col_blocks, WT)

    def attend_row(pair):
        return window_attention(pair[0], pair[1], w_qkv, w_out, rel_bias)
    attended = lax.map(attend_row, (win_all, label_all)).reshape(row_blocks * col_blocks, WT, D)
    window_grid = from_windows(attended, NLAT, NLON)
    taller_back = jnp.concatenate([window_grid[:, NLAT - WLAT:], window_grid], axis=1)
    wider_back = jnp.concatenate([taller_back[:, :, NLON - WLON:], taller_back], axis=2)
    restored = lax.dynamic_slice(wider_back, (zero_index, WLAT - lat_shift, WLON - lon_shift, zero_index), (LEVELS, NLAT, NLON, D))
    tok_blocks = fine_tokens.reshape(LEVELS, row_blocks, WLAT, NLON, D).transpose(1, 0, 2, 3, 4)
    res_blocks = restored.reshape(LEVELS, row_blocks, WLAT, NLON, D).transpose(1, 0, 2, 3, 4)

    def fine_row(pair):
        return fine_block(pair[0], pair[1], w_up, w_down)
    fine_blocks = lax.map(fine_row, (tok_blocks, res_blocks))
    fine_out = fine_blocks.transpose(1, 0, 2, 3, 4).reshape(LEVELS, NLAT, NLON, D)
    merged = fine_out.reshape(LEVELS, NLAT // 2, 2, NLON // 2, 2, D).transpose(0, 1, 3, 2, 4, 5)
    merged = merged.reshape(LEVELS, NLAT // 2, NLON // 2, 4 * D)
    half_blocks = NLAT // 2 // (WLAT // 2)
    merged_blocks = merged.reshape(LEVELS, half_blocks, WLAT // 2, NLON // 2, 4 * D).transpose(1, 0, 2, 3, 4)

    def middle_row(piece):
        return middle_block(piece, w_merge, w_inner, w_outer)
    middle_blocks = lax.map(middle_row, merged_blocks)
    middle = middle_blocks.transpose(1, 0, 2, 3, 4).reshape(LEVELS, NLAT // 2, NLON // 2, D2)
    return (fine_out, middle)
```

```python
import jax
import jax.numpy as jnp
from jax import lax
from jax.experimental import pallas as pl
from jax.experimental.pallas import tpu as pltpu
from jax.sharding import PartitionSpec as P

MESH = pl.DeviceIdType.MESH
F32 = jnp.float32
BF16 = jnp.bfloat16
LOG2E = 1.4426950408889634
ROOT_HALF = 0.7071067811865476

D = 512
FF = 2048
D2 = 1024
FF2 = 4096
HEADS = 8
WT = 144
ROWS = 24
COLS = 48
RIM = 16
WIN_LANES = HEADS * 128 + HEADS * 16
NT = (((1,), (1,)), ((), ()))


def mm(a, b):
    return jnp.dot(a, b, preferred_element_type=F32)


def mm_nt(a, b):
    return lax.dot_general(a, b, NT, preferred_element_type=F32)


def layer_norm(values):
    average = jnp.mean(values, axis=-1, keepdims=True)
    centered = values - average
    spread = jnp.mean(centered * centered, axis=-1, keepdims=True)
    return (centered * lax.rsqrt(spread + 1e-05)).astype(BF16)


def gelu(values):
    return (values * (0.5 + 0.5 * lax.erf(values * ROOT_HALF))).astype(BF16)


def iota(shape, dim):
    return lax.broadcasted_iota(jnp.int32, shape, dim)


def place():
    lat, lon = lax.axis_index("lat"), lax.axis_index("lon")
    return dict(zl=lat // 4, y=lat % 4, x=lon // 4, zh=(lon // 2) % 2, c=lon % 2)


def device(at, **changed):
    at = {**at, **changed}
    return {"lat": at["zl"] * 4 + at["y"], "lon": at["x"] * 4 + at["zh"] * 2 + at["c"]}


class Copies:
    def __init__(self, send, recv, local):
        self.send, self.recv, self.local = send, recv, local
        self.sent, self.landing, self.kept, self.count = [], {}, {}, 0

    def to(self, role, src, dst, mine, target):
        at = self.count
        self.count += 1
        copy = pltpu.make_async_remote_copy(
            src_ref=src,
            dst_ref=dst,
            send_sem=self.send.at[at],
            recv_sem=self.recv.at[at],
            device_id=target,
            device_id_type=MESH,
        )
        copy.start()
        self.sent.append(copy)
        self.landing[role] = pltpu.make_async_remote_copy(
            src_ref=mine,
            dst_ref=mine,
            send_sem=self.send.at[at],
            recv_sem=self.recv.at[at],
            device_id=target,
            device_id_type=MESH,
        )

    def arrived(self, role):
        self.landing.pop(role).wait_recv()

    def load(self, name, src, dst):
        copy = pltpu.make_async_copy(src, dst, self.local.at[len(self.kept)])
        copy.start()
        self.kept[name] = copy

    def loaded(self, name):
        self.kept[name].wait()

    def finish(self):
        for copy in self.sent:
            copy.wait_send()


def gather_steps(copies, at, sources, fulls):
    x, zh, c, y = at["x"], at["zh"], at["c"], at["y"]
    parity = y % 2
    east, west = (x + 1) % 4, (x + 3) % 4
    pair_one = y + 1 - 2 * parity
    pair_two = (y + 3 + 2 * parity) % 4
    pairs = (device(at, y=pair_one), device(at, y=pair_two))
    to_east, to_west = device(at, x=east), device(at, x=west)
    across = device(at, zh=1 - zh, zl=1 - at["zl"])
    sibling = device(at, c=1 - c)

    def shard(dx, dh=0, dc=0):
        return ((x + dx) % 4) * 4 + ((zh + dh) % 2) * 2 + (c + dc) % 2

    def build(m):
        src, full = sources[m], fulls[m]
        depth = src.shape[0]
        half, quarter = depth // 2, depth // 4

        def part(which, side=None, sub=None):
            start = which * depth
            if side is None:
                return full.at[pl.ds(pl.multiple_of(start, depth), depth)]
            start = start + ((parity + side) % 2) * half
            if sub is None:
                return full.at[pl.ds(pl.multiple_of(start, half), half)]
            return full.at[pl.ds(pl.multiple_of(start + sub * quarter, quarter), quarter)]

        def own(side=None):
            if side is None:
                return src
            return src.at[pl.ds(pl.multiple_of(((parity + side) % 2) * half, half), half)]

        def send(role, source, which_there, which_here, target, side=None, sub=None, side_here=None):
            side_here = side if side_here is None else side_here
            copies.to(
                (m,) + role,
                source,
                part(which_there, side, sub),
                part(which_here, side_here, sub),
                target,
            )

        me = shard(0)

        def swap(dx, dh, sub):
            which = shard(dx, dh)
            send(("y", dx, dh, sub), part(which, 0, sub), which, which, pairs[sub], 0, sub, 1)

        def spread(dh):
            which = shard(0, dh)
            source = own(0) if dh == 0 else part(which, 0)
            send(("x", 3, dh), source, which, shard(3, dh), to_east, 0)
            send(("x", 1, dh), source, which, shard(1, dh), to_west, 0)

        def relay(dh):
            copies.arrived((m, "x", 3, dh))
            send(("x2", dh, 0), part(shard(3, dh), 0, 0), shard(3, dh), shard(2, dh), to_east, 0, 0)
            copies.arrived((m, "x", 1, dh))
            send(("x2", dh, 1), part(shard(1, dh), 0, 1), shard(1, dh), shard(2, dh), to_west, 0, 1)
            for sub in (0, 1):
                swap(3, dh, sub)
                swap(1, dh, sub)

        def far(dh):
            for sub in (0, 1):
                copies.arrived((m, "x2", dh, sub))
                swap(2, dh, sub)

        def start():
            spread(0)
            send(("z", 0), own(0), me, shard(0, 1), across, 0)
            send(("z", 1), own(1), me, shard(0, 1), across, 1)
            send(("d", 0, 0), own(), me, shard(0, 0, 1), sibling)
            copies.load(("own", m), src, part(me))

        def across_step():
            copies.arrived((m, "z", 0))
            spread(1)

        def to_sibling(dx, dh):
            which = shard(dx, dh)
            send(("d", dx, dh), part(which), which, shard(dx, dh, 1), sibling)

        def close(dh):
            if dh == 1:
                copies.arrived((m, "z", 1))
                to_sibling(0, 1)
            for dx in (3, 1, 2):
                for sub in (0, 1):
                    copies.arrived((m, "y", dx, dh, sub))
                to_sibling(dx, dh)

        def last():
            for dh in (0, 1):
                for dx in range(4):
                    copies.arrived((m, "d", dx, dh))
            copies.loaded(("own", m))

        return [
            start,
            lambda: (relay(0), across_step()),
            lambda: far(0),
            lambda: relay(1),
            lambda: far(1),
            lambda: close(0),
            lambda: close(1),
            last,
        ]

    return [build(0), build(1)]


def kernel(
    shift_lat,
    shift_lon,
    tokens,
    bias_in,
    w_qkv,
    w_out,
    w_up,
    w_down,
    w_merge,
    w_inner,
    w_outer,
    fine_hbm,
    middle_hbm,
    wide,
    south,
    east,
    corner,
    qkv_v,
    wq_t,
    wv_t,
    out_v,
    up_v,
    down_v,
    merge_v,
    inner_v,
    outer_v,
    bias_raw,
    bias_v,
    xs,
    ks,
    cs,
    att,
    back,
    fine_v,
    normed_v,
    merged_v,
    coarse_v,
    acc_v,
    send_sem,
    recv_sem,
    local_sem,
):
    at = place()
    lat, lon = lax.axis_index("lat"), lax.axis_index("lon")
    n_lat, n_lon = lax.axis_size("lat"), lax.axis_size("lon")
    up_lat, down_lat = (lat + n_lat - 1) % n_lat, (lat + 1) % n_lat
    west_lon, east_lon = (lon + n_lon - 1) % n_lon, (lon + 1) % n_lon
    north_dev, south_dev = {"lat": up_lat, "lon": lon}, {"lat": down_lat, "lon": lon}
    west_dev, east_dev = {"lat": lat, "lon": west_lon}, {"lat": lat, "lon": east_lon}
    nw_dev, se_dev = {"lat": up_lat, "lon": west_lon}, {"lat": down_lat, "lon": east_lon}
    parity = at["y"] % 2
    friends = [
        north_dev,
        south_dev,
        west_dev,
        east_dev,
        nw_dev,
        se_dev,
        device(at, x=(at["x"] + 1) % 4),
        device(at, x=(at["x"] + 3) % 4),
        device(at, y=at["y"] + 1 - 2 * parity),
        device(at, y=(at["y"] + 3 + 2 * parity) % 4),
        device(at, zh=1 - at["zh"], zl=1 - at["zl"]),
        device(at, c=1 - at["c"]),
    ]
    copies = Copies(send_sem, recv_sem, local_sem)
    copies.load("tokens", tokens, wide.at[:, pl.ds(0, ROWS), pl.ds(0, COLS)])
    copies.load("qkv", w_qkv, qkv_v)
    copies.load("bias", bias_in, bias_raw)
    copies.load("out", w_out, out_v)
    barrier = pltpu.get_barrier_semaphore()
    for friend in friends:
        pl.semaphore_signal(barrier, inc=1, device_id=friend, device_id_type=MESH)
    pl.semaphore_wait(barrier, len(friends))

    copies.to("east", tokens.at[:, :, pl.ds(0, RIM)], east, east, west_dev)
    copies.to("south", tokens.at[:, pl.ds(0, 6)], south, south, north_dev)
    copies.to("corner", tokens.at[:, pl.ds(0, 6), pl.ds(0, RIM)], corner, corner, nw_dev)
    inner_steps, outer_steps = gather_steps(copies, at, (w_inner, w_outer), (inner_v, outer_v))
    inner_steps[0]()
    copies.load("up", w_up, up_v)
    copies.load("down", w_down, down_v)
    copies.load("merge", w_merge, merge_v)

    a = shift_lat[0]
    b = shift_lon[0]

    r, k = iota((192, 256), 0), iota((192, 256), 1)
    wc = (r >= 48).astype(jnp.int32) + (r >= 96).astype(jnp.int32) + (r >= 144).astype(jnp.int32)
    r2 = r - 48 * wc
    s = (r2 >= 12).astype(jnp.int32) + (r2 >= 24).astype(jnp.int32) + (r2 >= 36).astype(jnp.int32)
    perm_in = jnp.where(k == 64 * s + b + 12 * wc + r2 - 12 * s, 1.0, 0.0).astype(BF16)

    r, k = iota((192, 240), 0), iota((192, 240), 1)
    s = (r >= 48).astype(jnp.int32) + (r >= 96).astype(jnp.int32) + (r >= 144).astype(jnp.int32)
    from_col = r - 48 * s - b + 12
    wcp = sum((from_col >= 12 * i).astype(jnp.int32) for i in range(1, 5))
    perm_out = jnp.where(k == 36 * wcp + from_col + 12 * s, 1.0, 0.0).astype(BF16)

    copies.loaded("qkv")
    wq_t[...] = qkv_v[:, 0:D].T
    wv_t[...] = qkv_v[:, 2 * D : 3 * D].T
    copies.loaded("bias")
    for h in range(HEADS):
        bias_v[0, :, 128 * h : 128 * h + 128] = bias_raw[h, 0:128, :].T * LOG2E
    rest = jnp.concatenate([bias_raw[h, 128:144, :] for h in range(HEADS)], axis=0)
    bias_v[0, :, 1024:1152] = rest.T * LOG2E

    key_at = iota((WT, WIN_LANES), 0)
    lane = iota((WT, WIN_LANES), 1)
    query_at = jnp.where(lane < 1024, lane & 127, 128 + (lane & 15))
    edge = jnp.where(lat == n_lat - 1, 12 * (6 - a), 1000)

    def label(token):
        return (jnp.where(token >= 72, token - 72, token) >= edge).astype(jnp.int32)

    bias_v[1] = jnp.where(label(key_at) == label(query_at), bias_v[0], -1e30)

    rim_mask = (iota((D, 128), 0) >> 6) == (iota((D, 128), 1) >> 4)

    zeros_east = jnp.zeros((RIM, D), BF16)
    zeros_south = jnp.zeros((COLS, D), BF16)

    def clear(i, carry):
        for l in (0, 1):
            wide[l, i, COLS : COLS + RIM, :] = zeros_east
        return carry

    lax.fori_loop(0, ROWS + 6, clear, 0)

    def clear_south(i, carry):
        for l in (0, 1):
            wide[l, ROWS + i, 0:COLS, :] = zeros_south
        return carry

    lax.fori_loop(0, 6, clear_south, 0)
    copies.loaded("tokens")
    copies.loaded("out")

    def windows_in(wr, first, count, slot):
        for g in range(3):
            strips = []
            for i in range(4 * g, 4 * g + 4):
                strips.append(wide[i // 6, a + 6 * wr + i % 6])
            moved = mm(perm_in[48 * first : 48 * (first + count)], jnp.concatenate(strips, axis=0))
            moved = layer_norm(moved)
            for n in range(count):
                xs[slot + n, 48 * g : 48 * g + 48, :] = moved[48 * n : 48 * n + 48]

    def attend(n, masked):
        xw = xs[n]
        kw = ks[n]
        tail = xw[128:144]
        ext = jnp.concatenate([xw[0:128]] + [tail] * 8, axis=0)
        q_t = (mm_nt(wq_t[...], ext) * (0.125 * LOG2E)).astype(BF16)
        v_t = mm_nt(wv_t[...], xw).astype(BF16)
        zero = jnp.zeros((64, 128), BF16)
        main = []
        for p in range(4):
            qa = q_t[128 * p : 128 * p + 64, 0:128]
            qb = q_t[128 * p + 64 : 128 * p + 128, 0:128]
            diag = jnp.concatenate(
                [jnp.concatenate([qa, zero], axis=1), jnp.concatenate([zero, qb], axis=1)], axis=0
            )
            scores = mm(kw[:, 128 * p : 128 * p + 128], diag)
            scores = scores + bias_v[masked, :, 256 * p : 256 * p + 256]
            top = jnp.max(scores, axis=0, keepdims=True)
            exponent = jnp.exp2(scores - top)
            scale = 1.0 / jnp.sum(exponent, axis=0, keepdims=True)
            both = mm(v_t[128 * p : 128 * p + 128], exponent.astype(BF16)) * scale
            main.append(both[0:64, 0:128])
            main.append(both[64:128, 128:256])
        q_rest = jnp.where(rim_mask, q_t[:, 128:256], jnp.zeros((D, 128), BF16))
        scores = mm(kw, q_rest) + bias_v[masked, :, 1024:1152]
        top = jnp.max(scores, axis=0, keepdims=True)
        exponent = jnp.exp2(scores - top)
        scale = 1.0 / jnp.sum(exponent, axis=0, keepdims=True)
        last = mm(v_t, exponent.astype(BF16)) * scale
        last = jnp.where(rim_mask, last, 0.0).T
        rest_rows = sum(last[16 * h : 16 * h + 16] for h in range(1, HEADS)) + last[0:16]
        cs[n, 0:128, :] = jnp.concatenate(main, axis=0).T.astype(BF16)
        cs[n, 128:144, :] = rest_rows.astype(BF16)

    def batch(count, masked):
        ks[0:count] = mm(xs[0:count].reshape(count * WT, D), qkv_v[:, D : 2 * D]).astype(BF16).reshape(count, WT, D)

        def one(n, carry):
            attend(n, masked)
            return carry

        lax.fori_loop(0, count, one, 0)
        return mm(cs[0:count].reshape(count * WT, D), out_v[...]).astype(BF16).reshape(count, WT, D)

    def inside(wr, carry):
        windows_in(wr, 0, 3, 0)
        att[wr + 1, 1:4] = batch(3, 0)
        return carry

    lax.fori_loop(0, 1, inside, 0)
    inner_steps[1]()
    outer_steps[0]()
    lax.fori_loop(1, 3, inside, 0)
    inner_steps[2]()
    inner_steps[3]()

    copies.arrived("east")
    copies.arrived("south")
    copies.arrived("corner")

    def place_east(i, carry):
        for l in (0, 1):
            wide[l, i, COLS : COLS + RIM, :] = east[l, i]
        return carry

    lax.fori_loop(0, ROWS, place_east, 0)

    def place_south(i, carry):
        for l in (0, 1):
            wide[l, ROWS + i, 0:COLS, :] = south[l, i]
            wide[l, ROWS + i, COLS : COLS + RIM, :] = corner[l, i]
        return carry

    lax.fori_loop(0, 6, place_south, 0)

    for wr in range(3):
        windows_in(wr, 3, 1, wr)
    done = batch(3, 0)
    for wr in range(3):
        att[wr + 1, 4] = done[wr]
    copies.to("left", att.at[pl.ds(1, 3), 4], att.at[pl.ds(1, 3), 0], att.at[pl.ds(1, 3), 0], east_dev)
    inner_steps[4]()
    windows_in(3, 0, 4, 0)
    att[4, 1:5] = batch(4, 1)
    copies.to("left_low", att.at[4, 4], att.at[4, 0], att.at[4, 0], east_dev)
    copies.to("above", att.at[4, pl.ds(1, 4)], att.at[0, pl.ds(1, 4)], att.at[0, pl.ds(1, 4)], south_dev)
    copies.to("above_left", att.at[4, 4], att.at[0, 0], att.at[0, 0], se_dev)
    outer_steps[1]()
    inner_steps[5]()

    copies.loaded("up")
    copies.loaded("down")
    for role in ("left", "left_low", "above", "above_left"):
        copies.arrived(role)

    def put_back(wr, carry):
        for g in range(3):
            rows = jnp.concatenate([att[wr, w, 48 * g : 48 * g + 48, :] for w in range(5)], axis=0)
            moved = mm(perm_out, rows).astype(BF16)
            for n, i in enumerate(range(4 * g, 4 * g + 4)):
                back[i // 6, 6 * wr + i % 6] = moved[48 * n : 48 * n + 48]
        return carry

    lax.fori_loop(0, 5, put_back, 0)
    outer_steps[2]()
    inner_steps[6]()

    tile = 12

    def feed_forward(t, carry):
        l, r0 = t // 2, (t % 2) * tile
        own_rows = wide[l, pl.ds(r0, tile), 0:COLS, :].reshape(tile * COLS, D).astype(F32)
        residual = own_rows + back[l, pl.ds(r0 + 6 - a, tile)].reshape(tile * COLS, D).astype(F32)
        normed_v[...] = layer_norm(residual)
        total = residual
        for n in range(4):
            hidden = gelu(mm(normed_v[...], up_v[:, 512 * n : 512 * n + 512]))
            total = total + mm(hidden, down_v[512 * n : 512 * n + 512, :])
        fine_v[l, pl.ds(r0, tile)] = total.astype(BF16).reshape(tile, COLS, D)
        return carry

    lax.fori_loop(0, 2, feed_forward, 0)
    outer_steps[3]()
    outer_steps[4]()
    copies.load("fine0", fine_v.at[0], fine_hbm.at[0])
    lax.fori_loop(2, 4, feed_forward, 0)
    outer_steps[5]()
    copies.load("fine1", fine_v.at[1], fine_hbm.at[1])

    r, k = iota((192, 192), 0), iota((192, 192), 1)
    corner_at = (r >= 48).astype(jnp.int32) + (r >= 96).astype(jnp.int32) + (r >= 144).astype(jnp.int32)
    r2 = r - 48 * corner_at
    ii = (r2 >= 24).astype(jnp.int32)
    jj = r2 - 24 * ii
    perm_merge = jnp.where(
        k == 48 * (2 * ii + (corner_at >> 1)) + 2 * jj + (corner_at & 1), 1.0, 0.0
    ).astype(BF16)
    copies.loaded("merge")

    def merge(l, carry):
        def group(g, inner_carry):
            rows = fine_v[l, pl.ds(4 * g, 4)].reshape(192, D)
            moved = mm(perm_merge, rows)
            joined = jnp.concatenate([moved[48 * n : 48 * n + 48] for n in range(4)], axis=1)
            merged_v[pl.ds(pl.multiple_of(48 * g, 48), 48), :] = layer_norm(joined)
            return inner_carry

        lax.fori_loop(0, 6, group, 0)
        coarse = mm(merged_v[...], merge_v[...]).astype(BF16).astype(F32)
        rows = pl.ds(pl.multiple_of(288 * l, 288), 288)
        acc_v[rows, :] = coarse
        coarse_v[rows, :] = layer_norm(coarse)
        return carry

    lax.fori_loop(0, 2, merge, 0)
    inner_steps[7]()
    outer_steps[6]()
    outer_steps[7]()

    def middle(n, carry):
        cut = pl.ds(pl.multiple_of(1024 * n, 1024), 1024)
        hidden = gelu(mm(coarse_v[...], inner_v[:, cut]))
        acc_v[...] += mm(hidden, outer_v[cut, :])
        return carry

    lax.fori_loop(0, 4, middle, 0)
    middle_hbm[...] = acc_v[...].astype(BF16)
    copies.loaded("fine0")
    copies.loaded("fine1")
    copies.finish()


def on_device(
    fine_tokens,
    shift_lat,
    shift_lon,
    rel_bias,
    w_qkv,
    w_out,
    w_up,
    w_down,
    w_merge,
    w_inner,
    w_outer,
):
    hbm = pl.BlockSpec(memory_space=pl.ANY)
    smem = pl.BlockSpec(memory_space=pltpu.SMEM)
    vmem = pl.BlockSpec(memory_space=pltpu.VMEM)
    fine, middle = pl.pallas_call(
        kernel,
        out_shape=(
            jax.ShapeDtypeStruct((2, ROWS, COLS, D), BF16),
            jax.ShapeDtypeStruct((576, D2), BF16),
        ),
        in_specs=[smem, smem] + [hbm] * 9,
        out_specs=(hbm, vmem),
        scratch_shapes=[
            pltpu.VMEM((2, ROWS + 6, COLS + RIM, D), BF16),
            pltpu.VMEM((2, 6, COLS, D), BF16),
            pltpu.VMEM((2, ROWS, RIM, D), BF16),
            pltpu.VMEM((2, 6, RIM, D), BF16),
            pltpu.VMEM((D, 3 * D), BF16),
            pltpu.VMEM((D, D), BF16),
            pltpu.VMEM((D, D), BF16),
            pltpu.VMEM((D, D), BF16),
            pltpu.VMEM((D, FF), BF16),
            pltpu.VMEM((FF, D), BF16),
            pltpu.VMEM((4 * D, D2), BF16),
            pltpu.VMEM((D2, FF2), BF16),
            pltpu.VMEM((FF2, D2), BF16),
            pltpu.VMEM((HEADS, WT, WT), F32),
            pltpu.VMEM((2, WT, WIN_LANES), F32),
            pltpu.VMEM((4, WT, D), BF16),
            pltpu.VMEM((4, WT, D), BF16),
            pltpu.VMEM((4, WT, D), BF16),
            pltpu.VMEM((5, 5, WT, D), BF16),
            pltpu.VMEM((2, ROWS + 6, COLS, D), BF16),
            pltpu.VMEM((2, ROWS, COLS, D), BF16),
            pltpu.VMEM((576, D), BF16),
            pltpu.VMEM((288, 4 * D), BF16),
            pltpu.VMEM((576, D2), BF16),
            pltpu.VMEM((576, D2), F32),
            pltpu.SemaphoreType.DMA((80,)),
            pltpu.SemaphoreType.DMA((80,)),
            pltpu.SemaphoreType.DMA((16,)),
        ],
        compiler_params=pltpu.CompilerParams(
            collective_id=0, has_side_effects=True, vmem_limit_bytes=62 * 2**20
        ),
    )(shift_lat, shift_lon, fine_tokens, rel_bias, w_qkv, w_out, w_up, w_down, w_merge, w_inner, w_outer)
    return fine, middle.reshape(2, ROWS // 2, COLS // 2, D2)


def solution(mesh):
    whole = P()
    in_specs = (P(None, "lat", "lon", None),) + (whole,) * 8 + (P("lon", None), P("lon", None))
    out_specs = (P(None, "lat", "lon", None), P(None, "lat", "lon", None))
    return jax.shard_map(
        on_device, mesh=mesh, in_specs=in_specs, out_specs=out_specs, check_vma=False
    )
```

```python
import jax
import jax.numpy as jnp
from jax import lax
from jax.experimental import pallas as pl
from jax.experimental.pallas import tpu as pltpu
from jax.sharding import PartitionSpec as P

MESH = pl.DeviceIdType.MESH
F32 = jnp.float32
BF16 = jnp.bfloat16
LOG2E = 1.4426950408889634
ROOT_HALF = 0.7071067811865476

D = 512
FF = 2048
D2 = 1024
FF2 = 4096
HEADS = 8
WT = 144
ROWS = 24
COLS = 48
RIM = 16
WIN_LANES = HEADS * 128 + HEADS * 16
NT = (((1,), (1,)), ((), ()))


def mm(a, b):
    return jnp.dot(a, b, preferred_element_type=F32)


def mm_nt(a, b):
    return lax.dot_general(a, b, NT, preferred_element_type=F32)


def layer_norm(values):
    average = jnp.mean(values, axis=-1, keepdims=True)
    centered = values - average
    spread = jnp.mean(centered * centered, axis=-1, keepdims=True)
    return (centered * lax.rsqrt(spread + 1e-05)).astype(BF16)


def gelu(values):
    return (values * (0.5 + 0.5 * lax.erf(values * ROOT_HALF))).astype(BF16)


def iota(shape, dim):
    return lax.broadcasted_iota(jnp.int32, shape, dim)


def place():
    lat, lon = lax.axis_index("lat"), lax.axis_index("lon")
    return dict(zl=lat // 4, y=lat % 4, x=lon // 4, zh=(lon // 2) % 2, c=lon % 2)


def device(at, **changed):
    at = {**at, **changed}
    return {"lat": at["zl"] * 4 + at["y"], "lon": at["x"] * 4 + at["zh"] * 2 + at["c"]}


class Copies:
    def __init__(self, send, recv, local):
        self.send, self.recv, self.local = send, recv, local
        self.sent, self.landing, self.kept, self.count = [], {}, {}, 0

    def to(self, role, src, dst, mine, target, when=None):
        at = self.count
        self.count += 1

        def describe(source, destination):
            return pltpu.make_async_remote_copy(
                src_ref=source,
                dst_ref=destination,
                send_sem=self.send.at[at],
                recv_sem=self.recv.at[at],
                device_id=target,
                device_id_type=MESH,
            )

        self.only(when, lambda: describe(src, dst).start())
        self.sent.append((when, lambda: describe(src, dst).wait_send()))
        self.landing[role] = lambda: describe(mine, mine).wait_recv()

    def only(self, when, action):
        if when is None:
            action()
        else:
            pl.when(when)(action)

    def arrived(self, role, when=None):
        self.only(when, self.landing.pop(role))

    def load(self, name, src, dst):
        copy = pltpu.make_async_copy(src, dst, self.local.at[len(self.kept)])
        copy.start()
        self.kept[name] = copy

    def loaded(self, name):
        self.kept[name].wait()

    def finish(self):
        for when, action in self.sent:
            self.only(when, action)


def gather_steps(copies, at, sources, fulls):
    x, zh, c, y = at["x"], at["zh"], at["c"], at["y"]
    parity = y % 2
    east, west = (x + 1) % 4, (x + 3) % 4
    pair_one = y + 1 - 2 * parity
    pair_two = (y + 3 + 2 * parity) % 4
    pairs = (device(at, y=pair_one), device(at, y=pair_two))
    to_east, to_west = device(at, x=east), device(at, x=west)
    across = device(at, zh=1 - zh, zl=1 - at["zl"])
    sibling = device(at, c=1 - c)

    def shard(dx, dh=0, dc=0):
        return ((x + dx) % 4) * 4 + ((zh + dh) % 2) * 2 + (c + dc) % 2

    def build(m):
        src, full = sources[m], fulls[m]
        depth = src.shape[0]
        half, quarter = depth // 2, depth // 4

        def part(which, side=None, sub=None):
            start = which * depth
            if side is None:
                return full.at[pl.ds(pl.multiple_of(start, depth), depth)]
            start = start + ((parity + side) % 2) * half
            if sub is None:
                return full.at[pl.ds(pl.multiple_of(start, half), half)]
            return full.at[pl.ds(pl.multiple_of(start + sub * quarter, quarter), quarter)]

        def own(side=None):
            if side is None:
                return src
            return src.at[pl.ds(pl.multiple_of(((parity + side) % 2) * half, half), half)]

        def send(role, source, which_there, which_here, target, side=None, sub=None, side_here=None):
            side_here = side if side_here is None else side_here
            copies.to(
                (m,) + role,
                source,
                part(which_there, side, sub),
                part(which_here, side_here, sub),
                target,
            )

        me = shard(0)

        def swap(dx, dh, sub):
            which = shard(dx, dh)
            send(("y", dx, dh, sub), part(which, 0, sub), which, which, pairs[sub], 0, sub, 1)

        def spread(dh):
            which = shard(0, dh)
            source = own(0) if dh == 0 else part(which, 0)
            send(("x", 3, dh), source, which, shard(3, dh), to_east, 0)
            send(("x", 1, dh), source, which, shard(1, dh), to_west, 0)

        def relay(dh):
            copies.arrived((m, "x", 3, dh))
            send(("x2", dh, 0), part(shard(3, dh), 0, 0), shard(3, dh), shard(2, dh), to_east, 0, 0)
            copies.arrived((m, "x", 1, dh))
            send(("x2", dh, 1), part(shard(1, dh), 0, 1), shard(1, dh), shard(2, dh), to_west, 0, 1)
            for sub in (0, 1):
                swap(3, dh, sub)
                swap(1, dh, sub)

        def far(dh):
            for sub in (0, 1):
                copies.arrived((m, "x2", dh, sub))
                swap(2, dh, sub)

        def start():
            spread(0)
            send(("z", 0), own(0), me, shard(0, 1), across, 0)
            send(("z", 1), own(1), me, shard(0, 1), across, 1)
            send(("d", 0, 0), own(), me, shard(0, 0, 1), sibling)
            copies.load(("own", m), src, part(me))

        def across_step():
            copies.arrived((m, "z", 0))
            spread(1)

        def to_sibling(dx, dh):
            which = shard(dx, dh)
            send(("d", dx, dh), part(which), which, shard(dx, dh, 1), sibling)

        def close(dh):
            if dh == 1:
                copies.arrived((m, "z", 1))
                to_sibling(0, 1)
            for dx in (3, 1, 2):
                for sub in (0, 1):
                    copies.arrived((m, "y", dx, dh, sub))
                to_sibling(dx, dh)

        def last():
            for dh in (0, 1):
                for dx in range(4):
                    copies.arrived((m, "d", dx, dh))
            copies.loaded(("own", m))

        return dict(
            start=start,
            relay0=lambda: relay(0),
            across=across_step,
            far0=lambda: far(0),
            relay1=lambda: relay(1),
            far1=lambda: far(1),
            close0=lambda: close(0),
            close1=lambda: close(1),
            last=last,
        )

    return [build(0), build(1)]


def kernel(
    shift_lat,
    shift_lon,
    tokens,
    bias_in,
    w_qkv,
    w_out,
    w_up,
    w_down,
    w_merge,
    w_inner,
    w_outer,
    fine_hbm,
    middle_hbm,
    wide,
    south,
    east,
    corner,
    east_relay,
    left_relay,
    qkv_v,
    wq_t,
    wv_t,
    out_v,
    up_v,
    down_v,
    merge_v,
    inner_v,
    outer_v,
    bias_raw,
    bias_v,
    xs,
    ks,
    cs,
    att,
    back,
    fine_v,
    normed_v,
    merged_v,
    coarse_v,
    acc_v,
    send_sem,
    recv_sem,
    local_sem,
):
    at = place()
    lat, lon = lax.axis_index("lat"), lax.axis_index("lon")
    n_lat, n_lon = lax.axis_size("lat"), lax.axis_size("lon")
    up_lat, down_lat = (lat + n_lat - 1) % n_lat, (lat + 1) % n_lat
    west_lon, east_lon = (lon + n_lon - 1) % n_lon, (lon + 1) % n_lon
    north_dev, south_dev = {"lat": up_lat, "lon": lon}, {"lat": down_lat, "lon": lon}
    nw_dev, se_dev = {"lat": up_lat, "lon": west_lon}, {"lat": down_lat, "lon": east_lon}
    parity = at["y"] % 2
    friends = [
        north_dev,
        south_dev,
        nw_dev,
        se_dev,
        device(at, x=(at["x"] + 1) % 4),
        device(at, x=(at["x"] + 3) % 4),
        device(at, y=at["y"] + 1 - 2 * parity),
        device(at, y=(at["y"] + 3 + 2 * parity) % 4),
        device(at, zh=1 - at["zh"], zl=1 - at["zl"]),
        device(at, c=1 - at["c"]),
        device(at, zl=1 - at["zl"]),
    ]
    core, other = at["c"], 1 - at["c"]
    onward = jnp.where(core == 0, 3, 1)
    stay_x, next_x = at["x"], (at["x"] + onward) % 4
    over_a = device(
        at, c=other, zh=1 - at["zh"], zl=1 - at["zl"], x=jnp.where(at["zh"] == core, next_x, stay_x)
    )
    over_b = device(at, c=other, zl=1 - at["zl"], x=jnp.where(at["zh"] == core, stay_x, next_x))
    friends.append(over_a)
    friends.append(device(at, c=other, zl=1 - at["zl"]))
    friends.append(device(at, c=other, zl=1 - at["zl"], x=next_x))
    sibling = device(at, c=other)
    by_a = device(at, zh=1 - at["zh"], zl=1 - at["zl"])
    by_b = device(at, zl=1 - at["zl"])
    first_core, second_core = core == 0, core == 1
    copies = Copies(send_sem, recv_sem, local_sem)
    copies.load("tokens", tokens, wide.at[:, pl.ds(0, ROWS), pl.ds(0, COLS)])
    copies.load("qkv", w_qkv, qkv_v)
    copies.load("bias", bias_in, bias_raw)
    copies.load("out", w_out, out_v)
    barrier = pltpu.get_barrier_semaphore()
    for friend in friends:
        pl.semaphore_signal(barrier, inc=1, device_id=friend, device_id_type=MESH)
    pl.semaphore_wait(barrier, len(friends))

    for l, by in ((0, by_b), (1, by_a)):
        rim = tokens.at[l, :, pl.ds(0, RIM)]
        copies.to(("hop", l), rim, east_relay.at[l], east_relay.at[l], by, first_core)
    for l in (0, 1):
        rim = tokens.at[l, :, pl.ds(0, RIM)]
        copies.to(("near", l), rim, east.at[l], east.at[l], sibling, second_core)
    copies.to("south", tokens.at[:, pl.ds(0, 5)], south, south, north_dev)
    copies.to("corner", tokens.at[:, pl.ds(0, 5), pl.ds(0, RIM)], corner, corner, nw_dev)
    inner, outer = gather_steps(copies, at, (w_inner, w_outer), (inner_v, outer_v))
    inner["start"]()
    copies.load("up", w_up, up_v)
    copies.load("down", w_down, down_v)
    copies.load("merge", w_merge, merge_v)

    a = shift_lat[0]
    b = shift_lon[0]

    r, k = iota((192, 256), 0), iota((192, 256), 1)
    wc = (r >= 48).astype(jnp.int32) + (r >= 96).astype(jnp.int32) + (r >= 144).astype(jnp.int32)
    r2 = r - 48 * wc
    s = (r2 >= 12).astype(jnp.int32) + (r2 >= 24).astype(jnp.int32) + (r2 >= 36).astype(jnp.int32)
    perm_in = jnp.where(k == 64 * s + b + 12 * wc + r2 - 12 * s, 1.0, 0.0).astype(BF16)

    copies.loaded("qkv")
    wq_t[...] = qkv_v[:, 0:D].T
    wv_t[...] = qkv_v[:, 2 * D : 3 * D].T
    copies.loaded("bias")
    for h in range(HEADS):
        bias_v[0, :, 128 * h : 128 * h + 128] = bias_raw[h, 0:128, :].T * LOG2E
    rest = jnp.concatenate([bias_raw[h, 128:144, :] for h in range(HEADS)], axis=0)
    bias_v[0, :, 1024:1152] = rest.T * LOG2E

    key_at = iota((WT, WIN_LANES), 0)
    lane = iota((WT, WIN_LANES), 1)
    query_at = jnp.where(lane < 1024, lane & 127, 128 + (lane & 15))
    edge = jnp.where(lat == n_lat - 1, 12 * (6 - a), 1000)

    def label(token):
        return (jnp.where(token >= 72, token - 72, token) >= edge).astype(jnp.int32)

    bias_v[1] = jnp.where(label(key_at) == label(query_at), bias_v[0], -1e30)

    rim_mask = (iota((D, 128), 0) >> 6) == (iota((D, 128), 1) >> 4)

    zeros_east = jnp.zeros((RIM, D), BF16)
    zeros_south = jnp.zeros((COLS, D), BF16)

    def clear(i, carry):
        for l in (0, 1):
            wide[l, i, COLS : COLS + RIM, :] = zeros_east
        return carry

    lax.fori_loop(0, ROWS + 6, clear, 0)

    def clear_south(i, carry):
        for l in (0, 1):
            wide[l, ROWS + i, 0:COLS, :] = zeros_south
        return carry

    lax.fori_loop(0, 6, clear_south, 0)
    copies.loaded("tokens")
    copies.loaded("out")

    def windows_in(wr, first, count, slot):
        for g in range(3):
            strips = []
            for i in range(4 * g, 4 * g + 4):
                strips.append(wide[i // 6, a + 6 * wr + i % 6])
            moved = mm(perm_in[48 * first : 48 * (first + count)], jnp.concatenate(strips, axis=0))
            moved = layer_norm(moved)
            for n in range(count):
                xs[slot + n, 48 * g : 48 * g + 48, :] = moved[48 * n : 48 * n + 48]

    def attend(n, masked):
        xw = xs[n]
        kw = ks[n]
        tail = xw[128:144]
        ext = jnp.concatenate([xw[0:128]] + [tail] * 8, axis=0)
        q_t = (mm_nt(wq_t[...], ext) * (0.125 * LOG2E)).astype(BF16)
        v_t = mm_nt(wv_t[...], xw).astype(BF16)
        zero = jnp.zeros((64, 128), BF16)
        main = []
        for p in range(4):
            qa = q_t[128 * p : 128 * p + 64, 0:128]
            qb = q_t[128 * p + 64 : 128 * p + 128, 0:128]
            diag = jnp.concatenate(
                [jnp.concatenate([qa, zero], axis=1), jnp.concatenate([zero, qb], axis=1)], axis=0
            )
            scores = mm(kw[:, 128 * p : 128 * p + 128], diag)
            scores = scores + bias_v[masked, :, 256 * p : 256 * p + 256]
            top = jnp.max(scores, axis=0, keepdims=True)
            exponent = jnp.exp2(scores - top)
            scale = 1.0 / jnp.sum(exponent, axis=0, keepdims=True)
            both = mm(v_t[128 * p : 128 * p + 128], exponent.astype(BF16)) * scale
            main.append(both[0:64, 0:128])
            main.append(both[64:128, 128:256])
        q_rest = jnp.where(rim_mask, q_t[:, 128:256], jnp.zeros((D, 128), BF16))
        scores = mm(kw, q_rest) + bias_v[masked, :, 1024:1152]
        top = jnp.max(scores, axis=0, keepdims=True)
        exponent = jnp.exp2(scores - top)
        scale = 1.0 / jnp.sum(exponent, axis=0, keepdims=True)
        last = mm(v_t, exponent.astype(BF16)) * scale
        last = jnp.where(rim_mask, last, 0.0).T
        rest_rows = sum(last[16 * h : 16 * h + 16] for h in range(1, HEADS)) + last[0:16]
        cs[n, 0:128, :] = jnp.concatenate(main, axis=0).T.astype(BF16)
        cs[n, 128:144, :] = rest_rows.astype(BF16)

    def batch(count, masks, ticks):
        ks[0:count] = (
            mm(xs[0:count].reshape(count * WT, D), qkv_v[:, D : 2 * D])
            .astype(BF16)
            .reshape(count, WT, D)
        )
        for n in range(count):
            attend(n, masks[n])
            for tick in ticks[n]:
                tick()
        return mm(cs[0:count].reshape(count * WT, D), out_v[...]).astype(BF16).reshape(count, WT, D)

    def inside(wr, ticks):
        windows_in(wr, 0, 3, 0)
        att[wr + 1, 1:4] = batch(3, (0, 0, 0), ticks)

    def pass_west():
        for l, target in ((0, over_a), (1, over_b)):
            copies.arrived(("hop", l), first_core)
            copies.to(("far", l), east_relay.at[l], east.at[l], east.at[l], target, first_core)

    def pass_east(name, start, count, target):
        copies.arrived(("left_hop", name), second_core)
        here = att.at[pl.ds(1 + start, count), 0]
        source = left_relay.at[pl.ds(start, count)]
        copies.to(("left_far", name), source, here, here, target, second_core)

    inside(0, ([outer["start"]], [pass_west], [inner["relay0"]]))
    inside(1, ([inner["across"]], [], [inner["far0"]]))

    for l in (0, 1):
        copies.arrived(("near", l), first_core)
        copies.arrived(("far", l), second_core)

    def place_east(i, carry):
        for l in (0, 1):
            wide[l, i, COLS : COLS + RIM, :] = east[l, i]
        return carry

    lax.fori_loop(0, ROWS, place_east, 0)
    for wr in range(3):
        windows_in(wr, 3, 1, wr)
    done = batch(3, (0, 0, 0), ([outer["relay0"]], [inner["relay1"]], [outer["across"]]))
    for wr in range(3):
        att[wr + 1, 4] = done[wr]

    def send_left(name, start, count, by):
        there = left_relay.at[pl.ds(start, count)]
        rows = att.at[pl.ds(1 + start, count), 4]
        copies.to(("left_hop", name), rows, there, there, by, second_core)
        left = att.at[pl.ds(1 + start, count), 0]
        copies.to(("left_near", name), rows, left, left, sibling, first_core)

    send_left(0, 0, 2, by_b)
    send_left(1, 2, 1, by_a)

    copies.arrived("south")
    copies.arrived("corner")

    def place_south(i, carry):
        for l in (0, 1):
            wide[l, ROWS + i, 0:COLS, :] = south[l, i]
            wide[l, ROWS + i, COLS : COLS + RIM, :] = corner[l, i]
        return carry

    lax.fori_loop(0, 5, place_south, 0)
    windows_in(3, 0, 4, 0)
    att[4, 1:5] = batch(
        4,
        (1, 1, 1, 1),
        ([inner["far1"]], [inner["close0"]], [outer["far0"]], [lambda: pass_east(0, 0, 2, over_a)]),
    )
    above = att.at[0, pl.ds(1, 4)]
    copies.to("above", att.at[4, pl.ds(1, 4)], above, above, south_dev)
    copies.to("above_left", att.at[4, 4], att.at[0, 0], att.at[0, 0], se_dev)
    send_left(2, 3, 1, by_a)

    inside(
        2,
        (
            [lambda: pass_east(1, 2, 1, over_b), outer["relay1"]],
            [inner["close1"]],
            [lambda: pass_east(2, 3, 1, over_b)],
        ),
    )

    def put_back(wr, permutation, first, last, col, width):
        for g in range(3):
            rows = jnp.concatenate(
                [att[wr, w, 48 * g : 48 * g + 48, :] for w in range(first, last)], axis=0
            )
            moved = mm(permutation, rows).astype(BF16)
            for n, i in enumerate(range(4 * g, 4 * g + 4)):
                back[i // 6, 6 * wr + i % 6, col : col + width, :] = moved[width * n : width * n + width]

    def returning(col, width, first, last):
        shape = (4 * width, 48 * (last - first))
        r, k = iota(shape, 0), iota(shape, 1)
        s = sum((r >= width * i).astype(jnp.int32) for i in range(1, 4))
        from_col = r - width * s + col - b + 12
        wcp = sum((from_col >= 12 * i).astype(jnp.int32) for i in range(1, 5))
        return jnp.where(k + 48 * first == 36 * wcp + from_col + 12 * s, 1.0, 0.0).astype(BF16)

    copies.loaded("up")
    copies.loaded("down")

    def feed_forward(residual):
        normed_v[...] = layer_norm(residual)
        total = residual
        for n in range(4):
            hidden = gelu(mm(normed_v[...], up_v[:, 512 * n : 512 * n + 512]))
            total = total + mm(hidden, down_v[512 * n : 512 * n + 512, :])
        return total.astype(BF16)

    def residual_of(l, row, count, col, width):
        tokens_in = wide[l, row : row + count, col : col + width, :].astype(F32)
        returned = back[l, pl.ds(row + 6 - a, count), col : col + width, :].astype(F32)
        return (tokens_in + returned).reshape(count * width, D)

    inland = returning(16, 32, 1, 5)

    def put_inland(wr, carry):
        put_back(wr, inland, 1, 5, 16, 32)
        return carry

    lax.fori_loop(1, 5, put_inland, 0)

    def forward_inland(l, carry):
        fine_v[l, 6:24, 16:48, :] = feed_forward(residual_of(l, 6, 18, 16, 32)).reshape(18, 32, D)
        return carry

    lax.fori_loop(0, 2, forward_inland, 0)

    for name in range(3):
        copies.arrived(("left_near", name), second_core)
        copies.arrived(("left_far", name), first_core)
    coast = returning(0, 16, 0, 3)

    def put_coast(wr, carry):
        put_back(wr, coast, 0, 3, 0, 16)
        return carry

    lax.fori_loop(1, 5, put_coast, 0)
    rows = [residual_of(l, 6, 18, 0, 16) for l in (0, 1)]
    done = feed_forward(jnp.concatenate(rows, axis=0)).reshape(2, 18, 16, D)
    for l in (0, 1):
        fine_v[l, 6:24, 0:16, :] = done[l]
    outer["far1"]()
    copies.load("fine0", fine_v.at[:, pl.ds(6, 18)], fine_hbm.at[:, pl.ds(6, 18)])

    copies.arrived("above")
    copies.arrived("above_left")
    put_back(0, returning(0, 48, 0, 5), 0, 5, 0, 48)
    rows = [residual_of(l, 0, 6, 0, 48) for l in (0, 1)]
    done = feed_forward(jnp.concatenate(rows, axis=0)).reshape(2, 6, 48, D)
    for l in (0, 1):
        fine_v[l, 0:6] = done[l]
    outer["close0"]()
    copies.load("fine1", fine_v.at[:, pl.ds(0, 6)], fine_hbm.at[:, pl.ds(0, 6)])

    r, k = iota((192, 192), 0), iota((192, 192), 1)
    corner_at = (r >= 48).astype(jnp.int32) + (r >= 96).astype(jnp.int32) + (r >= 144).astype(jnp.int32)
    r2 = r - 48 * corner_at
    ii = (r2 >= 24).astype(jnp.int32)
    jj = r2 - 24 * ii
    perm_merge = jnp.where(
        k == 48 * (2 * ii + (corner_at >> 1)) + 2 * jj + (corner_at & 1), 1.0, 0.0
    ).astype(BF16)
    copies.loaded("merge")

    def merge(g, carry):
        for l in (0, 1):
            moved = mm(perm_merge, fine_v[l, pl.ds(4 * g, 4)].reshape(192, D))
            joined = jnp.concatenate([moved[48 * n : 48 * n + 48] for n in range(4)], axis=1)
            rows = pl.ds(pl.multiple_of(288 * l + 48 * g, 48), 48)
            merged_v[rows, :] = layer_norm(joined)
        return carry

    lax.fori_loop(0, 3, merge, 0)
    outer["close1"]()
    lax.fori_loop(3, 6, merge, 0)
    coarse = mm(merged_v[...], merge_v[...]).astype(BF16).astype(F32)
    acc_v[...] = coarse
    coarse_v[...] = layer_norm(coarse)
    inner["last"]()
    outer["last"]()

    def middle(n, carry):
        cut = pl.ds(pl.multiple_of(1024 * n, 1024), 1024)
        hidden = gelu(mm(coarse_v[...], inner_v[:, cut]))
        acc_v[...] += mm(hidden, outer_v[cut, :])
        return carry

    lax.fori_loop(0, 4, middle, 0)
    middle_hbm[...] = acc_v[...].astype(BF16)
    copies.loaded("fine0")
    copies.loaded("fine1")
    copies.finish()


def on_device(
    fine_tokens,
    shift_lat,
    shift_lon,
    rel_bias,
    w_qkv,
    w_out,
    w_up,
    w_down,
    w_merge,
    w_inner,
    w_outer,
):
    hbm = pl.BlockSpec(memory_space=pl.ANY)
    smem = pl.BlockSpec(memory_space=pltpu.SMEM)
    vmem = pl.BlockSpec(memory_space=pltpu.VMEM)
    fine, middle = pl.pallas_call(
        kernel,
        out_shape=(
            jax.ShapeDtypeStruct((2, ROWS, COLS, D), BF16),
            jax.ShapeDtypeStruct((576, D2), BF16),
        ),
        in_specs=[smem, smem] + [hbm] * 9,
        out_specs=(hbm, vmem),
        scratch_shapes=[
            pltpu.VMEM((2, ROWS + 6, COLS + RIM, D), BF16),
            pltpu.VMEM((2, 5, COLS, D), BF16),
            pltpu.VMEM((2, ROWS, RIM, D), BF16),
            pltpu.VMEM((2, 5, RIM, D), BF16),
            pltpu.VMEM((2, ROWS, RIM, D), BF16),
            pltpu.VMEM((4, WT, D), BF16),
            pltpu.VMEM((D, 3 * D), BF16),
            pltpu.VMEM((D, D), BF16),
            pltpu.VMEM((D, D), BF16),
            pltpu.VMEM((D, D), BF16),
            pltpu.VMEM((D, FF), BF16),
            pltpu.VMEM((FF, D), BF16),
            pltpu.VMEM((4 * D, D2), BF16),
            pltpu.VMEM((D2, FF2), BF16),
            pltpu.VMEM((FF2, D2), BF16),
            pltpu.VMEM((HEADS, WT, WT), F32),
            pltpu.VMEM((2, WT, WIN_LANES), F32),
            pltpu.VMEM((4, WT, D), BF16),
            pltpu.VMEM((4, WT, D), BF16),
            pltpu.VMEM((4, WT, D), BF16),
            pltpu.VMEM((5, 5, WT, D), BF16),
            pltpu.VMEM((2, ROWS + 6, COLS, D), BF16),
            pltpu.VMEM((2, ROWS, COLS, D), BF16),
            pltpu.VMEM((576, D), BF16),
            pltpu.VMEM((576, 4 * D), BF16),
            pltpu.VMEM((576, D2), BF16),
            pltpu.VMEM((576, D2), F32),
            pltpu.SemaphoreType.DMA((80,)),
            pltpu.SemaphoreType.DMA((80,)),
            pltpu.SemaphoreType.DMA((16,)),
        ],
        compiler_params=pltpu.CompilerParams(
            collective_id=0, has_side_effects=True, vmem_limit_bytes=62 * 2**20
        ),
    )(shift_lat, shift_lon, fine_tokens, rel_bias, w_qkv, w_out, w_up, w_down, w_merge, w_inner, w_outer)
    return fine, middle.reshape(2, ROWS // 2, COLS // 2, D2)


def solution(mesh):
    whole = P()
    in_specs = (P(None, "lat", "lon", None),) + (whole,) * 8 + (P("lon", None), P("lon", None))
    out_specs = (P(None, "lat", "lon", None), P(None, "lat", "lon", None))
    return jax.shard_map(
        on_device, mesh=mesh, in_specs=in_specs, out_specs=out_specs, check_vma=False
    )
```

```python
import jax
import jax.numpy as jnp
from jax import lax
from jax.experimental import pallas as pl
from jax.experimental.pallas import tpu as pltpu
from jax.sharding import PartitionSpec as P

MESH = pl.DeviceIdType.MESH
F32 = jnp.float32
BF16 = jnp.bfloat16
LOG2E = 1.4426950408889634
ROOT_HALF = 0.7071067811865476

D = 512
FF = 2048
D2 = 1024
FF2 = 4096
HEADS = 8
WT = 144
ROWS = 24
COLS = 48
RIM = 16
WIN_LANES = HEADS * 128 + HEADS * 16
NT = (((1,), (1,)), ((), ()))


def mm(a, b):
    return jnp.dot(a, b, preferred_element_type=F32)


def mm_nt(a, b):
    return lax.dot_general(a, b, NT, preferred_element_type=F32)


def layer_norm(values):
    average = jnp.mean(values, axis=-1, keepdims=True)
    centered = values - average
    spread = jnp.mean(centered * centered, axis=-1, keepdims=True)
    return (centered * lax.rsqrt(spread + 1e-05)).astype(BF16)


def gelu(values):
    return (values * (0.5 + 0.5 * lax.erf(values * ROOT_HALF))).astype(BF16)


def iota(shape, dim):
    return lax.broadcasted_iota(jnp.int32, shape, dim)


def place():
    lat, lon = lax.axis_index("lat"), lax.axis_index("lon")
    return dict(zl=lat // 4, y=lat % 4, x=lon // 4, zh=(lon // 2) % 2, c=lon % 2)


def device(at, **changed):
    at = {**at, **changed}
    return {"lat": at["zl"] * 4 + at["y"], "lon": at["x"] * 4 + at["zh"] * 2 + at["c"]}


class Copies:
    def __init__(self, send, recv, local):
        self.send, self.recv, self.local = send, recv, local
        self.sent, self.landing, self.kept, self.count = [], {}, {}, 0

    def to(self, role, src, dst, mine, target, when=None):
        at = self.count
        self.count += 1

        def describe(source, destination):
            return pltpu.make_async_remote_copy(
                src_ref=source,
                dst_ref=destination,
                send_sem=self.send.at[at],
                recv_sem=self.recv.at[at],
                device_id=target,
                device_id_type=MESH,
            )

        self.only(when, lambda: describe(src, dst).start())
        self.sent.append((when, lambda: describe(src, dst).wait_send()))
        self.landing[role] = lambda: describe(mine, mine).wait_recv()

    def only(self, when, action):
        if when is None:
            action()
        else:
            pl.when(when)(action)

    def arrived(self, role, when=None):
        self.only(when, self.landing.pop(role))

    def load(self, name, src, dst):
        copy = pltpu.make_async_copy(src, dst, self.local.at[len(self.kept)])
        copy.start()
        self.kept[name] = copy

    def loaded(self, name):
        self.kept[name].wait()

    def finish(self):
        for when, action in self.sent:
            self.only(when, action)


def gather_steps(copies, at, sources, fulls):
    x, zh, c, y = at["x"], at["zh"], at["c"], at["y"]
    parity = y % 2
    east, west = (x + 1) % 4, (x + 3) % 4
    pair_one = y + 1 - 2 * parity
    pair_two = (y + 3 + 2 * parity) % 4
    pairs = (device(at, y=pair_one), device(at, y=pair_two))
    to_east, to_west = device(at, x=east), device(at, x=west)
    across = device(at, zh=1 - zh, zl=1 - at["zl"])
    sibling = device(at, c=1 - c)

    def shard(dx, dh=0, dc=0):
        return ((x + dx) % 4) * 4 + ((zh + dh) % 2) * 2 + (c + dc) % 2

    def build(m):
        src, full = sources[m], fulls[m]
        depth = src.shape[0]
        half, quarter = depth // 2, depth // 4

        def part(which, side=None, sub=None):
            start = which * depth
            if side is None:
                return full.at[pl.ds(pl.multiple_of(start, depth), depth)]
            start = start + ((parity + side) % 2) * half
            if sub is None:
                return full.at[pl.ds(pl.multiple_of(start, half), half)]
            return full.at[pl.ds(pl.multiple_of(start + sub * quarter, quarter), quarter)]

        def own(side=None):
            if side is None:
                return src
            return src.at[pl.ds(pl.multiple_of(((parity + side) % 2) * half, half), half)]

        def send(role, source, which_there, which_here, target, side=None, sub=None, side_here=None):
            side_here = side if side_here is None else side_here
            copies.to(
                (m,) + role,
                source,
                part(which_there, side, sub),
                part(which_here, side_here, sub),
                target,
            )

        me = shard(0)

        def swap(dx, dh, sub):
            which = shard(dx, dh)
            send(("y", dx, dh, sub), part(which, 0, sub), which, which, pairs[sub], 0, sub, 1)

        def spread(dh):
            which = shard(0, dh)
            source = own(0) if dh == 0 else part(which, 0)
            send(("x", 3, dh), source, which, shard(3, dh), to_east, 0)
            send(("x", 1, dh), source, which, shard(1, dh), to_west, 0)

        def relay(dh):
            copies.arrived((m, "x", 3, dh))
            send(("x2", dh, 0), part(shard(3, dh), 0, 0), shard(3, dh), shard(2, dh), to_east, 0, 0)
            copies.arrived((m, "x", 1, dh))
            send(("x2", dh, 1), part(shard(1, dh), 0, 1), shard(1, dh), shard(2, dh), to_west, 0, 1)
            for sub in (0, 1):
                swap(3, dh, sub)
                swap(1, dh, sub)

        def far(dh):
            for sub in (0, 1):
                copies.arrived((m, "x2", dh, sub))
                swap(2, dh, sub)

        def start():
            spread(0)
            send(("d", 0, 0), own(), me, shard(0, 0, 1), sibling)
            copies.load(("own", m), src, part(me))

        def over_z():
            send(("z", 0), own(0), me, shard(0, 1), across, 0)
            send(("z", 1), own(1), me, shard(0, 1), across, 1)

        def across_step():
            copies.arrived((m, "z", 0))
            spread(1)

        def to_sibling(dx, dh):
            which = shard(dx, dh)
            send(("d", dx, dh), part(which), which, shard(dx, dh, 1), sibling)

        def close(dh):
            if dh == 1:
                copies.arrived((m, "z", 1))
                to_sibling(0, 1)
            for dx in (3, 1, 2):
                for sub in (0, 1):
                    copies.arrived((m, "y", dx, dh, sub))
                to_sibling(dx, dh)

        def last():
            for dh in (0, 1):
                for dx in range(4):
                    copies.arrived((m, "d", dx, dh))
            copies.loaded(("own", m))

        return dict(
            start=start,
            over_z=over_z,
            relay0=lambda: relay(0),
            across=across_step,
            far0=lambda: far(0),
            relay1=lambda: relay(1),
            far1=lambda: far(1),
            close0=lambda: close(0),
            close1=lambda: close(1),
            last=last,
        )

    return [build(0), build(1)]


def kernel(
    shift_lat,
    shift_lon,
    tokens,
    bias_in,
    w_qkv,
    w_out,
    w_up,
    w_down,
    w_merge,
    w_inner,
    w_outer,
    fine_hbm,
    middle_hbm,
    wide,
    south,
    east,
    corner,
    east_relay,
    left_relay,
    qkv_v,
    wq_t,
    wv_t,
    out_v,
    up_v,
    down_v,
    merge_v,
    inner_v,
    outer_v,
    bias_raw,
    bias_v,
    xs,
    ks,
    cs,
    att,
    back,
    fine_v,
    normed_v,
    merged_v,
    coarse_v,
    acc_v,
    send_sem,
    recv_sem,
    local_sem,
):
    at = place()
    lat, lon = lax.axis_index("lat"), lax.axis_index("lon")
    n_lat = lax.axis_size("lat")
    up_lat, down_lat = (lat + n_lat - 1) % n_lat, (lat + 1) % n_lat
    n_lon = lax.axis_size("lon")
    west_lon, east_lon = (lon + n_lon - 1) % n_lon, (lon + 1) % n_lon
    nw_dev, se_dev = {"lat": up_lat, "lon": west_lon}, {"lat": down_lat, "lon": east_lon}
    north_dev, south_dev = {"lat": up_lat, "lon": lon}, {"lat": down_lat, "lon": lon}
    parity = at["y"] % 2
    friends = [
        north_dev,
        south_dev,
        nw_dev,
        se_dev,
        device(at, x=(at["x"] + 1) % 4),
        device(at, x=(at["x"] + 3) % 4),
        device(at, y=at["y"] + 1 - 2 * parity),
        device(at, y=(at["y"] + 3 + 2 * parity) % 4),
        device(at, zh=1 - at["zh"], zl=1 - at["zl"]),
        device(at, c=1 - at["c"]),
        device(at, zl=1 - at["zl"]),
    ]
    core, other = at["c"], 1 - at["c"]
    onward = jnp.where(core == 0, 3, 1)
    stay_x, next_x = at["x"], (at["x"] + onward) % 4
    over_a = device(
        at, c=other, zh=1 - at["zh"], zl=1 - at["zl"], x=jnp.where(at["zh"] == core, next_x, stay_x)
    )
    over_b = device(at, c=other, zl=1 - at["zl"], x=jnp.where(at["zh"] == core, stay_x, next_x))
    friends.append(over_a)
    friends.append(device(at, c=other, zl=1 - at["zl"]))
    friends.append(device(at, c=other, zl=1 - at["zl"], x=next_x))
    sibling = device(at, c=other)
    by_a = device(at, zh=1 - at["zh"], zl=1 - at["zl"])
    by_b = device(at, zl=1 - at["zl"])
    first_core, second_core = core == 0, core == 1
    copies = Copies(send_sem, recv_sem, local_sem)
    copies.load("tokens", tokens, wide.at[:, pl.ds(0, ROWS), pl.ds(0, COLS)])
    copies.load("qkv", w_qkv, qkv_v)
    copies.load("bias", bias_in, bias_raw)
    copies.load("out", w_out, out_v)
    barrier = pltpu.get_barrier_semaphore()
    for friend in friends:
        pl.semaphore_signal(barrier, inc=1, device_id=friend, device_id_type=MESH)
    pl.semaphore_wait(barrier, len(friends))

    for l, by in ((0, by_b), (1, by_a)):
        rim = tokens.at[l, :, pl.ds(0, RIM)]
        copies.to(("hop", l), rim, east_relay.at[l], east_relay.at[l], by, first_core)
    for l in (0, 1):
        rim = tokens.at[l, :, pl.ds(0, RIM)]
        copies.to(("near", l), rim, east.at[l], east.at[l], sibling, second_core)
    copies.to("south", tokens.at[:, pl.ds(0, 5)], south, south, north_dev)
    copies.to("corner", tokens.at[:, pl.ds(0, 5), pl.ds(0, RIM)], corner, corner, nw_dev)
    inner, outer = gather_steps(copies, at, (w_inner, w_outer), (inner_v, outer_v))
    inner["start"]()
    copies.load("up", w_up, up_v)
    copies.load("down", w_down, down_v)
    copies.load("merge", w_merge, merge_v)

    a = shift_lat[0]
    b = shift_lon[0]

    r, k = iota((192, 256), 0), iota((192, 256), 1)
    wc = (r >= 48).astype(jnp.int32) + (r >= 96).astype(jnp.int32) + (r >= 144).astype(jnp.int32)
    r2 = r - 48 * wc
    s = (r2 >= 12).astype(jnp.int32) + (r2 >= 24).astype(jnp.int32) + (r2 >= 36).astype(jnp.int32)
    perm_in = jnp.where(k == 64 * s + b + 12 * wc + r2 - 12 * s, 1.0, 0.0).astype(BF16)

    copies.loaded("qkv")
    wq_t[...] = qkv_v[:, 0:D].T
    wv_t[...] = qkv_v[:, 2 * D : 3 * D].T
    copies.loaded("bias")
    for h in range(HEADS):
        bias_v[0, :, 128 * h : 128 * h + 128] = bias_raw[h, 0:128, :].T * LOG2E
    rest = jnp.concatenate([bias_raw[h, 128:144, :] for h in range(HEADS)], axis=0)
    bias_v[0, :, 1024:1152] = rest.T * LOG2E

    key_at = iota((WT, WIN_LANES), 0)
    lane = iota((WT, WIN_LANES), 1)
    query_at = jnp.where(lane < 1024, lane & 127, 128 + (lane & 15))
    edge = jnp.where(lat == n_lat - 1, 12 * (6 - a), 1000)

    def label(token):
        return (jnp.where(token >= 72, token - 72, token) >= edge).astype(jnp.int32)

    bias_v[1] = jnp.where(label(key_at) == label(query_at), bias_v[0], -1e30)

    rim_mask = (iota((D, 128), 0) >> 6) == (iota((D, 128), 1) >> 4)

    zeros_east = jnp.zeros((RIM, D), BF16)
    zeros_south = jnp.zeros((COLS, D), BF16)

    def clear(i, carry):
        for l in (0, 1):
            wide[l, i, COLS : COLS + RIM, :] = zeros_east
        return carry

    lax.fori_loop(0, ROWS + 6, clear, 0)

    def clear_south(i, carry):
        for l in (0, 1):
            wide[l, ROWS + i, 0:COLS, :] = zeros_south
        return carry

    lax.fori_loop(0, 6, clear_south, 0)
    copies.loaded("tokens")
    copies.loaded("out")

    def windows_in(wr, first, count, slot):
        for g in range(3):
            strips = []
            for i in range(4 * g, 4 * g + 4):
                strips.append(wide[i // 6, a + 6 * wr + i % 6])
            moved = mm(perm_in[48 * first : 48 * (first + count)], jnp.concatenate(strips, axis=0))
            moved = layer_norm(moved)
            for n in range(count):
                xs[slot + n, 48 * g : 48 * g + 48, :] = moved[48 * n : 48 * n + 48]

    def attend(n, masked):
        xw = xs[n]
        kw = ks[n]
        tail = xw[128:144]
        ext = jnp.concatenate([xw[0:128]] + [tail] * 8, axis=0)
        q_t = (mm_nt(wq_t[...], ext) * (0.125 * LOG2E)).astype(BF16)
        v_t = mm_nt(wv_t[...], xw).astype(BF16)
        zero = jnp.zeros((64, 128), BF16)
        main = []
        for p in range(4):
            qa = q_t[128 * p : 128 * p + 64, 0:128]
            qb = q_t[128 * p + 64 : 128 * p + 128, 0:128]
            diag = jnp.concatenate(
                [jnp.concatenate([qa, zero], axis=1), jnp.concatenate([zero, qb], axis=1)], axis=0
            )
            scores = mm(kw[:, 128 * p : 128 * p + 128], diag)
            scores = scores + bias_v[masked, :, 256 * p : 256 * p + 256]
            top = jnp.max(scores, axis=0, keepdims=True)
            exponent = jnp.exp2(scores - top)
            scale = 1.0 / jnp.sum(exponent, axis=0, keepdims=True)
            both = mm(v_t[128 * p : 128 * p + 128], exponent.astype(BF16)) * scale
            main.append(both[0:64, 0:128])
            main.append(both[64:128, 128:256])
        q_rest = jnp.where(rim_mask, q_t[:, 128:256], jnp.zeros((D, 128), BF16))
        scores = mm(kw, q_rest) + bias_v[masked, :, 1024:1152]
        top = jnp.max(scores, axis=0, keepdims=True)
        exponent = jnp.exp2(scores - top)
        scale = 1.0 / jnp.sum(exponent, axis=0, keepdims=True)
        last = mm(v_t, exponent.astype(BF16)) * scale
        last = jnp.where(rim_mask, last, 0.0).T
        rest_rows = sum(last[16 * h : 16 * h + 16] for h in range(1, HEADS)) + last[0:16]
        cs[n, 0:128, :] = jnp.concatenate(main, axis=0).T.astype(BF16)
        cs[n, 128:144, :] = rest_rows.astype(BF16)

    def batch(count, masks, ticks):
        ks[0:count] = (
            mm(xs[0:count].reshape(count * WT, D), qkv_v[:, D : 2 * D])
            .astype(BF16)
            .reshape(count, WT, D)
        )
        for n in range(count):
            attend(n, masks[n])
            for tick in ticks[n]:
                tick()
        return mm(cs[0:count].reshape(count * WT, D), out_v[...]).astype(BF16).reshape(count, WT, D)

    def inside(wr, ticks):
        windows_in(wr, 0, 3, 0)
        att[wr + 1, 1:4] = batch(3, (0, 0, 0), ticks)

    def pass_west():
        for l, target in ((0, over_a), (1, over_b)):
            copies.arrived(("hop", l), first_core)
            copies.to(("far", l), east_relay.at[l], east.at[l], east.at[l], target, first_core)

    def pass_east(name, start, count, target):
        copies.arrived(("left_hop", name), second_core)
        here = att.at[pl.ds(1 + start, count), 0]
        source = left_relay.at[pl.ds(start, count)]
        copies.to(("left_far", name), source, here, here, target, second_core)

    inside(0, ([], [pass_west], [inner["over_z"], outer["start"]]))
    inside(1, ([inner["relay0"]], [], []))

    inside(2, ([inner["across"]], [inner["far0"], outer["over_z"]], [outer["relay0"]]))

    for l in (0, 1):
        copies.arrived(("near", l), first_core)
        copies.arrived(("far", l), second_core)

    def place_east(i, carry):
        for l in (0, 1):
            wide[l, i, COLS : COLS + RIM, :] = east[l, i]
        return carry

    lax.fori_loop(0, ROWS, place_east, 0)
    for wr in range(3):
        windows_in(wr, 3, 1, wr)
    done = batch(3, (0, 0, 0), ([inner["relay1"]], [outer["across"]], [inner["far1"]]))
    for wr in range(3):
        att[wr + 1, 4] = done[wr]

    def send_left(name, start, count, by):
        there = left_relay.at[pl.ds(start, count)]
        rows = att.at[pl.ds(1 + start, count), 4]
        copies.to(("left_hop", name), rows, there, there, by, second_core)
        left = att.at[pl.ds(1 + start, count), 0]
        copies.to(("left_near", name), rows, left, left, sibling, first_core)

    send_left(0, 0, 2, by_b)
    send_left(1, 2, 1, by_a)

    copies.arrived("south")
    copies.arrived("corner")

    def place_south(i, carry):
        for l in (0, 1):
            wide[l, ROWS + i, 0:COLS, :] = south[l, i]
            wide[l, ROWS + i, COLS : COLS + RIM, :] = corner[l, i]
        return carry

    lax.fori_loop(0, 5, place_south, 0)
    windows_in(3, 0, 4, 0)
    att[4, 1:5] = batch(
        4,
        (1, 1, 1, 1),
        ([inner["close0"]], [outer["far0"]], [lambda: pass_east(0, 0, 2, over_a)], [lambda: pass_east(1, 2, 1, over_b)]),
    )
    above = att.at[0, pl.ds(1, 4)]
    copies.to("above", att.at[4, pl.ds(1, 4)], above, above, south_dev)
    copies.to("above_left", att.at[4, 4], att.at[0, 0], att.at[0, 0], se_dev)
    send_left(2, 3, 1, by_a)

    def put_back(wr, permutation, first, last, col, width):
        for g in range(3):
            rows = jnp.concatenate(
                [att[wr, w, 48 * g : 48 * g + 48, :] for w in range(first, last)], axis=0
            )
            moved = mm(permutation, rows).astype(BF16)
            for n, i in enumerate(range(4 * g, 4 * g + 4)):
                back[i // 6, 6 * wr + i % 6, col : col + width, :] = moved[width * n : width * n + width]

    def returning(col, width, first, last):
        shape = (4 * width, 48 * (last - first))
        r, k = iota(shape, 0), iota(shape, 1)
        s = sum((r >= width * i).astype(jnp.int32) for i in range(1, 4))
        from_col = r - width * s + col - b + 12
        wcp = sum((from_col >= 12 * i).astype(jnp.int32) for i in range(1, 5))
        return jnp.where(k + 48 * first == 36 * wcp + from_col + 12 * s, 1.0, 0.0).astype(BF16)

    copies.loaded("up")
    copies.loaded("down")

    def feed_forward(residual):
        normed_v[...] = layer_norm(residual)
        total = residual
        for n in range(4):
            hidden = gelu(mm(normed_v[...], up_v[:, 512 * n : 512 * n + 512]))
            total = total + mm(hidden, down_v[512 * n : 512 * n + 512, :])
        return total.astype(BF16)

    def residual_of(l, row, count, col, width):
        tokens_in = wide[l, row : row + count, col : col + width, :].astype(F32)
        returned = back[l, pl.ds(row + 6 - a, count), col : col + width, :].astype(F32)
        return (tokens_in + returned).reshape(count * width, D)

    inland = returning(16, 32, 1, 5)

    def put_inland(wr, carry):
        put_back(wr, inland, 1, 5, 16, 32)
        return carry

    lax.fori_loop(1, 5, put_inland, 0)

    def forward_inland(l, carry):
        fine_v[l, 6:24, 16:48, :] = feed_forward(residual_of(l, 6, 18, 16, 32)).reshape(18, 32, D)
        return carry

    lax.fori_loop(0, 1, forward_inland, 0)
    pass_east(2, 3, 1, over_b)
    outer["relay1"]()
    lax.fori_loop(1, 2, forward_inland, 0)
    inner["close1"]()

    for name in range(3):
        copies.arrived(("left_near", name), second_core)
        copies.arrived(("left_far", name), first_core)
    coast = returning(0, 16, 0, 3)

    def put_coast(wr, carry):
        put_back(wr, coast, 0, 3, 0, 16)
        return carry

    lax.fori_loop(1, 5, put_coast, 0)
    rows = [residual_of(l, 6, 18, 0, 16) for l in (0, 1)]
    done = feed_forward(jnp.concatenate(rows, axis=0)).reshape(2, 18, 16, D)
    for l in (0, 1):
        fine_v[l, 6:24, 0:16, :] = done[l]
    outer["far1"]()
    copies.load("fine0", fine_v.at[:, pl.ds(6, 18)], fine_hbm.at[:, pl.ds(6, 18)])

    copies.arrived("above")
    copies.arrived("above_left")
    put_back(0, returning(0, 48, 0, 5), 0, 5, 0, 48)
    rows = [residual_of(l, 0, 6, 0, 48) for l in (0, 1)]
    done = feed_forward(jnp.concatenate(rows, axis=0)).reshape(2, 6, 48, D)
    for l in (0, 1):
        fine_v[l, 0:6] = done[l]
    outer["close0"]()
    copies.load("fine1", fine_v.at[:, pl.ds(0, 6)], fine_hbm.at[:, pl.ds(0, 6)])

    r, k = iota((192, 192), 0), iota((192, 192), 1)
    corner_at = (r >= 48).astype(jnp.int32) + (r >= 96).astype(jnp.int32) + (r >= 144).astype(jnp.int32)
    r2 = r - 48 * corner_at
    ii = (r2 >= 24).astype(jnp.int32)
    jj = r2 - 24 * ii
    perm_merge = jnp.where(
        k == 48 * (2 * ii + (corner_at >> 1)) + 2 * jj + (corner_at & 1), 1.0, 0.0
    ).astype(BF16)
    copies.loaded("merge")

    def merge(g, carry):
        for l in (0, 1):
            moved = mm(perm_merge, fine_v[l, pl.ds(4 * g, 4)].reshape(192, D))
            joined = jnp.concatenate([moved[48 * n : 48 * n + 48] for n in range(4)], axis=1)
            rows = pl.ds(pl.multiple_of(288 * l + 48 * g, 48), 48)
            merged_v[rows, :] = layer_norm(joined)
        return carry

    lax.fori_loop(0, 3, merge, 0)
    outer["close1"]()
    lax.fori_loop(3, 6, merge, 0)
    coarse = mm(merged_v[...], merge_v[...]).astype(BF16).astype(F32)
    acc_v[...] = coarse
    coarse_v[...] = layer_norm(coarse)
    inner["last"]()
    outer["last"]()

    def middle(n, carry):
        cut = pl.ds(pl.multiple_of(1024 * n, 1024), 1024)
        hidden = gelu(mm(coarse_v[...], inner_v[:, cut]))
        acc_v[...] += mm(hidden, outer_v[cut, :])
        return carry

    lax.fori_loop(0, 4, middle, 0)
    middle_hbm[...] = acc_v[...].astype(BF16)
    copies.loaded("fine0")
    copies.loaded("fine1")
    copies.finish()


def on_device(
    fine_tokens,
    shift_lat,
    shift_lon,
    rel_bias,
    w_qkv,
    w_out,
    w_up,
    w_down,
    w_merge,
    w_inner,
    w_outer,
):
    hbm = pl.BlockSpec(memory_space=pl.ANY)
    smem = pl.BlockSpec(memory_space=pltpu.SMEM)
    vmem = pl.BlockSpec(memory_space=pltpu.VMEM)
    fine, middle = pl.pallas_call(
        kernel,
        out_shape=(
            jax.ShapeDtypeStruct((2, ROWS, COLS, D), BF16),
            jax.ShapeDtypeStruct((576, D2), BF16),
        ),
        in_specs=[smem, smem] + [hbm] * 9,
        out_specs=(hbm, vmem),
        scratch_shapes=[
            pltpu.VMEM((2, ROWS + 6, COLS + RIM, D), BF16),
            pltpu.VMEM((2, 5, COLS, D), BF16),
            pltpu.VMEM((2, ROWS, RIM, D), BF16),
            pltpu.VMEM((2, 5, RIM, D), BF16),
            pltpu.VMEM((2, ROWS, RIM, D), BF16),
            pltpu.VMEM((4, WT, D), BF16),
            pltpu.VMEM((D, 3 * D), BF16),
            pltpu.VMEM((D, D), BF16),
            pltpu.VMEM((D, D), BF16),
            pltpu.VMEM((D, D), BF16),
            pltpu.VMEM((D, FF), BF16),
            pltpu.VMEM((FF, D), BF16),
            pltpu.VMEM((4 * D, D2), BF16),
            pltpu.VMEM((D2, FF2), BF16),
            pltpu.VMEM((FF2, D2), BF16),
            pltpu.VMEM((HEADS, WT, WT), F32),
            pltpu.VMEM((2, WT, WIN_LANES), F32),
            pltpu.VMEM((4, WT, D), BF16),
            pltpu.VMEM((4, WT, D), BF16),
            pltpu.VMEM((4, WT, D), BF16),
            pltpu.VMEM((5, 5, WT, D), BF16),
            pltpu.VMEM((2, ROWS + 6, COLS, D), BF16),
            pltpu.VMEM((2, ROWS, COLS, D), BF16),
            pltpu.VMEM((576, D), BF16),
            pltpu.VMEM((576, 4 * D), BF16),
            pltpu.VMEM((576, D2), BF16),
            pltpu.VMEM((576, D2), F32),
            pltpu.SemaphoreType.DMA((80,)),
            pltpu.SemaphoreType.DMA((80,)),
            pltpu.SemaphoreType.DMA((16,)),
        ],
        compiler_params=pltpu.CompilerParams(
            collective_id=0, has_side_effects=True, vmem_limit_bytes=62 * 2**20
        ),
    )(shift_lat, shift_lon, fine_tokens, rel_bias, w_qkv, w_out, w_up, w_down, w_merge, w_inner, w_outer)
    return fine, middle.reshape(2, ROWS // 2, COLS // 2, D2)


def solution(mesh):
    whole = P()
    in_specs = (P(None, "lat", "lon", None),) + (whole,) * 8 + (P("lon", None), P("lon", None))
    out_specs = (P(None, "lat", "lon", None), P(None, "lat", "lon", None))
    return jax.shard_map(
        on_device, mesh=mesh, in_specs=in_specs, out_specs=out_specs, check_vma=False
    )
```
